512 devices in a mesh: col: 128 (over y_lo, z, x, core), row: 4 (over y_hi).
Axes of the slice: x: 4, y: 8 (y_hi: 4, y_lo: 2; y = y_hi * 2 + y_lo), z: 8, core: 2. Of those that a mesh axis runs over, the one named last changes fastest.
Arguments:
- g2_block: bfloat16 [2048, 2, 131072], P('row', None, 'col'), may hold values from -6 to 6
- panel_slots: bfloat16 [128, 2, 2, 256, 2048], P('col', None, None, None, 'row'), may hold values from -0.125 to 0.125
- owners: int32 [2], replicated, may hold values from 0 to 127
- green_one: float32 [2, 400, 400], replicated, may hold values from -6 to 6
Outputs:
- rate: bfloat16 [256, 2, 2, 131072], P('row', None, None, 'col')
The draws below stay inside these ranges and needn't reach their ends.
All inputs are finite; a program needn't handle non-finite values.
Results may differ from the reference program's by a relative error of at most 0.012.
Values may be sent and summed in bfloat16 or wider, within the bound.
No kernel may reach another device: no remote copies, remote signals or barrier semaphores. Data moves between devices by JAX's collectives and lax.ppermute only.
A program may use at most 64 MiB of HBM per device.

```python
import jax
import jax.numpy as jnp
from jax import lax

NORB = 400
PW = 256
NPAN = 2
KR = 512
KTOT = 2048
COLS = 131072
N_COL = 128
N_ROW = 4


def levels(rng, dims, pieces, low, high):
    loudness = 1.0
    for dim, blocks in pieces:
        steps = jax.random.uniform(jax.random.fold_in(jax.random.fold_in(rng, 6), dim), (blocks,), jnp.float32, low / len(pieces), high / len(pieces))
        loudness = loudness * jnp.repeat(jnp.exp(steps), dims[dim] // blocks).reshape((-1,) + (1,) * (len(dims) - 1 - dim))
    return loudness


def centred(rng, shape, spread, reach, split=(), kind=jnp.bfloat16):
    loudness = levels(rng, shape, split, -0.22, 0.18) if split else 1.0
    array = jax.random.normal(rng, shape, jnp.float32) * spread * loudness
    return jnp.minimum(jnp.maximum(array, -reach), reach).astype(kind)


def setup_inputs(seed: int = 0) -> dict:
    key_list = jax.random.split(jax.random.key(seed), 5)
    g2_block = centred(key_list[0], (KTOT, 2, COLS), 1.0, 6.0, ((0, 4), (2, 128)))
    panel_slots = centred(key_list[1], (N_COL, NPAN, 2, PW, KTOT), KTOT ** -0.5, 0.125, ((0, 128), (4, 4)))
    owners = jax.random.randint(key_list[2], (NPAN,), 0, N_COL).astype(jnp.int32)
    green_one = centred(key_list[3], (2, NORB, NORB), 1.0, 6.0, (), jnp.float32)
    return {"g2_block": g2_block, "panel_slots": panel_slots, "owners": owners, "green_one": green_one}


def source_terms(owners, green_one, index):
    pairs = (2 * owners[index] + index) * PW + jnp.arange(PW, dtype=jnp.int32)
    first = pairs // NORB
    second = pairs % NORB
    columns = jnp.arange(COLS, dtype=jnp.int32)
    left_orb = columns // NORB
    right_orb = columns % NORB
    left_re = green_one[0][first[:, None], left_orb[None, :]]
    left_im = green_one[1][first[:, None], left_orb[None, :]]
    right_re = green_one[0][second[:, None], right_orb[None, :]]
    right_im = green_one[1][second[:, None], right_orb[None, :]]
    return left_re * right_re - left_im * right_im, left_re * right_im + left_im * right_re


def reference(g2_block, panel_slots, owners, green_one):
    results = []
    for index in range(NPAN):
        panel = panel_slots[owners[index], index]
        prod_re = jnp.zeros((PW, COLS), jnp.float32)
        prod_im = jnp.zeros((PW, COLS), jnp.float32)
        for slab in range(N_ROW):
            lower = slab * KR
            flat = g2_block[lower:lower + KR].reshape(KR, 2 * COLS)
            left = panel[:, :, lower:lower + KR].reshape(2 * PW, KR)
            full = jnp.dot(left, flat, preferred_element_type=jnp.float32)
            part_re = full[:PW, :COLS] - full[PW:, COLS:]
            part_im = full[:PW, COLS:] + full[PW:, :COLS]
            part_re = lax.optimization_barrier(part_re.astype(jnp.bfloat16)).astype(jnp.float32)
            part_im = lax.optimization_barrier(part_im.astype(jnp.bfloat16)).astype(jnp.float32)
            prod_re = prod_re + part_re
            prod_im = prod_im + part_im
        src_re, src_im = source_terms(owners, green_one, index)
        rate_re = prod_im + src_re
        rate_im = src_im - prod_re
        results.append(jnp.stack([rate_re, rate_im], axis=1))
    return jnp.stack(results, axis=1).astype(jnp.bfloat16)
```

```python
import jax
import jax.numpy as jnp
from jax import lax
from jax.sharding import Mesh, PartitionSpec as P

NPAN = 2
SIZES = {"y": 2, "z": 8, "x": 4, "core": 2, "row": 4}
COL = ("y", "z", "x", "core")
TILE = 8


def shift(array, axis, step):
    size = SIZES[axis]
    pairs = [(index, (index + step) % size) for index in range(size)]
    return lax.ppermute(array, axis, pairs)


def pick(array, index):
    return lax.dynamic_index_in_dim(array, index, 0, keepdims=False)


def scatter_line(array, axis, root):
    size = SIZES[axis]
    me = lax.axis_index(axis)
    away = (me - root) % size
    result = pick(array, me)
    for step in range(1, size):
        got = shift(pick(array, (me + step) % size), axis, step)
        result = jnp.where(away == step, got, result)
    return result


def gather_line(array, axis):
    size = SIZES[axis]
    me = lax.axis_index(axis)
    ring = [array] + [shift(array, axis, size - step) for step in range(1, size)]
    if size == 2:
        swapped = me == 1
        return jnp.stack([jnp.where(swapped, ring[1], ring[0]), jnp.where(swapped, ring[0], ring[1])])
    return lax.dynamic_slice_in_dim(jnp.stack(ring + ring[:-1]), (size - me) % size, size, 0)


def place(owner):
    core = owner % 2
    x = (owner // 2) % 4
    z = (owner // 8) % 8
    y = owner // 64
    return y, z, x, core


def spread_permutes(panel, owner):
    y, z, x, core = place(owner)
    half = scatter_line(panel.reshape(2, 4 * 8, TILE, -1), "core", core)
    quarter = scatter_line(half.reshape(4, 8, TILE, -1), "x", x)
    piece = scatter_line(quarter, "z", z)
    other = shift(piece, "y", 1)
    piece = jnp.where(lax.axis_index("y") == y, piece, other)
    line = gather_line(piece, "z")
    plane = gather_line(line, "x")
    return gather_line(plane, "core").reshape(panel.shape)


def spread_grouped(panel, owner):
    y, z, x, core = place(owner)
    half = scatter_line(panel.reshape(2, 8 * 4, TILE, -1), "core", core)
    got = lax.all_to_all(half, ("z", "x"), 0, 0, tiled=True)
    piece = pick(got, z * 4 + x)
    other = shift(piece, "y", 1)
    piece = jnp.where(lax.axis_index("y") == y, piece, other)
    plane = lax.all_gather(piece, ("z", "x"), axis=0)
    return gather_line(plane, "core").reshape(panel.shape)


def turned(panel):
    rows = panel.shape[1] // SIZES["row"]
    re, im = panel[0], panel[1]
    full = jnp.stack([jnp.concatenate([im, re], axis=1), jnp.concatenate([-re, im], axis=1)])
    return full.reshape(2, SIZES["row"], rows, full.shape[-1]).transpose(1, 0, 2, 3)


def reduce_permutes(left, right):
    row = lax.axis_index("row")
    rows = left.shape[2]

    def term(part):
        chunk = pick(left, part % 4).reshape(2 * rows, -1)
        return jnp.dot(chunk, right, preferred_element_type=jnp.float32).reshape(2, rows, -1)

    def small(array):
        return array.astype(jnp.bfloat16)

    far = small(term(row + 2))
    from_left = shift(far[0], "row", 1)
    from_right = shift(far[1], "row", -1)
    up = term(row + 1)
    down = term(row + 3)
    left_im = shift(small(up[1]), "row", 1)
    right_re = shift(small(down[0]), "row", -1)
    left_re = shift(small(up[0] + from_left.astype(jnp.float32)), "row", 1)
    right_im = shift(small(down[1] + from_right.astype(jnp.float32)), "row", -1)
    own = term(row)
    first = own[0] + left_re.astype(jnp.float32) + right_re.astype(jnp.float32)
    second = own[1] + left_im.astype(jnp.float32) + right_im.astype(jnp.float32)
    return first, second


def reduce_grouped(left, right):
    parts, _, rows, depth = left.shape
    full = jnp.dot(left.reshape(-1, depth), right, preferred_element_type=jnp.float32)
    full = full.astype(jnp.bfloat16).reshape(parts, 2 * rows, -1)
    mine = lax.psum_scatter(full, "row", scatter_dimension=0, tiled=True)
    mine = mine.reshape(2, rows, -1).astype(jnp.float32)
    return mine[0], mine[1]


def source(owners, green, index, rows, width):
    orbitals = green.shape[1]
    row0 = (2 * owners[index] + index) * (rows * SIZES["row"]) + lax.axis_index("row") * rows
    col0 = lax.axis_index(COL) * width
    i0, j0 = row0 // orbitals, row0 % orbitals
    k0, l0 = col0 // orbitals, col0 % orbitals
    corner = lax.dynamic_slice(green, (0, i0, k0), (2, 2, 4))
    next_row = (j0 + jnp.arange(rows) >= orbitals)[:, None]
    run = ((l0 + jnp.arange(width)) // orbitals)[None, :]

    def left(part):
        values = jnp.zeros((rows, width), jnp.float32)
        for step in range(4):
            pair = jnp.where(next_row, corner[part, 1, step], corner[part, 0, step])
            values = jnp.where(run == step, pair, values)
        return values

    twice = jnp.concatenate([green, green[:, :rows]], axis=1)
    strip = lax.dynamic_slice(twice, (0, j0, 0), (2, rows, orbitals))
    strip = jnp.concatenate([strip] * 4, axis=2)
    strip = lax.dynamic_slice(strip, (0, 0, l0), (2, rows, width))
    a_re, a_im = left(0), left(1)
    return a_re * strip[0] - a_im * strip[1], a_re * strip[1] + a_im * strip[0]


def shards(g2_block, panel_slots, owners, green_one):
    width = g2_block.shape[2]
    rows = panel_slots.shape[3] // SIZES["row"]
    right = g2_block.transpose(1, 0, 2).reshape(-1, width)
    first = turned(spread_permutes(panel_slots[0, 0], owners[0]))
    second = turned(spread_grouped(panel_slots[0, 1], owners[1]))
    sums = [reduce_permutes(first, right), reduce_grouped(second, right)]
    planes = []
    for index in range(NPAN):
        src = source(owners, green_one, index, rows, width)
        planes.append(jnp.stack([sums[index][0] + src[0], sums[index][1] + src[1]], axis=1))
    return jnp.stack(planes, axis=1).astype(jnp.bfloat16)


def solution(mesh):
    sizes = tuple(SIZES.values())
    fine = Mesh(mesh.devices.reshape(sizes), tuple(SIZES))
    return jax.shard_map(
        shards,
        mesh=fine,
        in_specs=(P("row", None, COL), P(COL, None, None, None, "row"), P(), P()),
        out_specs=P("row", None, None, COL),
        check_vma=False,
    )
```

```python
import jax
import jax.numpy as jnp
from jax import lax
from jax.sharding import Mesh, PartitionSpec as P

NPAN = 2
SIZES = {"y": 2, "z": 8, "x": 4, "core": 2, "row": 4}
COL = ("y", "z", "x", "core")
PLANE = ("x", "core")


def pick(array, index):
    return lax.dynamic_index_in_dim(array, index, 0, keepdims=False)


def to_all(array, axes, count):
    copies = jnp.broadcast_to(array[None], (count,) + array.shape)
    return lax.all_to_all(copies, axes, 0, 0, tiled=True)


def spread(panel, owner):
    depth = panel.shape[-1]
    inner = owner % 8
    z = (owner // 8) % 8
    y = owner // 64
    parts = lax.all_to_all(panel.reshape(8, -1, depth), PLANE, 0, 0, tiled=True)
    part = pick(parts, inner).reshape(8, -1, depth)
    pieces = lax.all_to_all(jnp.concatenate([part, part]), ("y", "z"), 0, 0, tiled=True)
    piece = pick(pieces, y * 8 + z)
    line = to_all(piece, "z", 8).reshape(-1, depth)
    return to_all(line, PLANE, 8).reshape(-1, depth)


def slab_product(panel, right):
    depth = panel.shape[-1]
    left = panel.reshape(2, -1, depth).transpose(1, 0, 2).reshape(-1, 2 * depth)
    return jnp.dot(left, right, preferred_element_type=jnp.float32).astype(jnp.bfloat16)


def reduce_row(product):
    rows = product.shape[0] // SIZES["row"]
    mine = lax.all_to_all(product.reshape(SIZES["row"], rows, -1), "row", 0, 0, tiled=True)
    return jnp.sum(mine.astype(jnp.float32), axis=0)


def chosen(index, count):
    return (index[:, None] == jnp.arange(count, dtype=jnp.int32)[None, :]).astype(jnp.float32)


def source(owners, green, rows, width):
    orbitals = green.shape[1]
    first = (2 * owners + jnp.arange(NPAN, dtype=jnp.int32)) * (rows * SIZES["row"])
    pairs = first[:, None] + lax.axis_index("row") * rows + jnp.arange(rows, dtype=jnp.int32)[None, :]
    pairs = pairs.reshape(-1)
    columns = lax.axis_index(COL) * width + jnp.arange(width, dtype=jnp.int32)

    def take(row_index, col_index):
        half = jnp.einsum("qi,cik->cqk", chosen(row_index, orbitals), green, precision="highest")
        return jnp.einsum("cqk,nk->cqn", half, chosen(col_index, orbitals), precision="highest")

    a = take(pairs // orbitals, columns // orbitals)
    b = take(pairs % orbitals, columns % orbitals)
    re = a[0] * b[0] - a[1] * b[1]
    im = a[0] * b[1] + a[1] * b[0]
    return jnp.stack([re, im], axis=1).reshape(NPAN, rows, 2, width)


def shards(g2_block, panel_slots, owners, green_one):
    width = g2_block.shape[2]
    rows = panel_slots.shape[3] // SIZES["row"]
    re, im = g2_block[:, 0], g2_block[:, 1]
    right = jnp.concatenate([jnp.concatenate([im, -re], axis=1), jnp.concatenate([re, im], axis=1)])
    panels = [spread(panel_slots[0, index], owners[index]) for index in range(NPAN)]
    products = [slab_product(panel, right) for panel in panels]
    green, last = lax.optimization_barrier((green_one, products[1]))
    src = source(owners, green, rows, width)
    sums = [reduce_row(products[0]), reduce_row(last)]
    planes = [sums[index].reshape(rows, 2, width) + src[index] for index in range(NPAN)]
    return jnp.stack(planes, axis=1).astype(jnp.bfloat16)


def solution(mesh):
    fine = Mesh(mesh.devices.reshape(tuple(SIZES.values())), tuple(SIZES))
    return jax.shard_map(
        shards,
        mesh=fine,
        in_specs=(P("row", None, COL), P(COL, None, None, None, "row"), P(), P()),
        out_specs=P("row", None, None, COL),
        check_vma=False,
    )
```

```python
import jax
import jax.numpy as jnp
from jax import lax
from jax.sharding import Mesh, PartitionSpec as P

NPAN = 2
SIZES = {"y": 2, "z": 8, "x": 4, "core": 2, "row": 4}
COL = ("y", "z", "x", "core")


def pick(array, index):
    return lax.dynamic_index_in_dim(array, index, 0, keepdims=False)


def shift(array, step):
    size = SIZES["row"]
    return lax.ppermute(array, "row", [(index, (index + step) % size) for index in range(size)])


def scatter(panels, owners):
    half = panels.shape[-1] // 2
    pieces = panels.reshape(NPAN, -1, 8, 2, half).transpose(1, 3, 0, 2, 4).reshape(-1, NPAN, 8, half)
    got = lax.all_to_all(pieces, COL, 0, 0, tiled=True)
    return [pick(got, owners[index])[index] for index in range(NPAN)]


def gather(piece):
    count = 2 * SIZES["y"] * SIZES["z"] * SIZES["x"]
    got = lax.all_to_all(jnp.broadcast_to(piece[None], (count,) + piece.shape), COL, 0, 0, tiled=True)
    return got.reshape(count // 2, 2, *piece.shape).transpose(0, 2, 1, 3).reshape(count * 4, -1)


def turned(panel):
    re, im = panel.reshape(2, -1, panel.shape[-1])
    full = jnp.stack([jnp.concatenate([im, re], axis=1), jnp.concatenate([-re, im], axis=1)])
    return full.reshape(2, SIZES["row"], -1, full.shape[-1]).transpose(1, 0, 2, 3)


def reduce_row(left, right):
    row = lax.axis_index("row")
    rows = left.shape[2]

    def term(step):
        part = pick(left, (row + step) % SIZES["row"]).reshape(2 * rows, -1)
        part = jnp.dot(part, right, preferred_element_type=jnp.float32)
        return part.astype(jnp.bfloat16).astype(jnp.float32).reshape(2, rows, -1)

    far = term(2).astype(jnp.bfloat16)
    from_left = shift(far[0], 1).astype(jnp.float32)
    from_right = shift(far[1], -1).astype(jnp.float32)
    up, down = term(1), term(3)
    up = jnp.stack([up[0] + from_left, up[1]]).astype(jnp.bfloat16)
    down = jnp.stack([down[0], down[1] + from_right]).astype(jnp.bfloat16)
    sent = (up, down)
    own = term(0)
    up = shift(up, 1).astype(jnp.float32)
    down = shift(down, -1).astype(jnp.float32)
    return own + up + down, sent


def chosen(index, count):
    return (index[:, None] == jnp.arange(count, dtype=jnp.int32)[None, :]).astype(jnp.float32)


def source(owners, green, rows, width):
    orbitals = green.shape[1]
    first = (2 * owners + jnp.arange(NPAN, dtype=jnp.int32)) * (rows * SIZES["row"])
    pairs = first[:, None] + lax.axis_index("row") * rows + jnp.arange(rows, dtype=jnp.int32)[None, :]
    pairs = pairs.reshape(-1)
    columns = lax.axis_index(COL) * width + jnp.arange(width, dtype=jnp.int32)

    def take(row_index, col_index):
        half = jnp.einsum("qi,cik->cqk", chosen(row_index, orbitals), green, precision="highest")
        return jnp.einsum("cqk,nk->cqn", half, chosen(col_index, orbitals), precision="highest")

    a = take(pairs // orbitals, columns // orbitals)
    b = take(pairs % orbitals, columns % orbitals)
    re = a[0] * b[0] - a[1] * b[1]
    im = a[0] * b[1] + a[1] * b[0]
    return jnp.stack([re, im]).reshape(2, NPAN, rows, width).transpose(1, 0, 2, 3)


def shards(g2_block, panel_slots, owners, green_one):
    width = g2_block.shape[2]
    rows = panel_slots.shape[3] // SIZES["row"]
    right = g2_block.transpose(1, 0, 2).reshape(-1, width)
    pieces = scatter(panel_slots[0], owners)
    panels = [gather(piece) for piece in pieces]
    first, sent = reduce_row(turned(panels[0]), right)
    second, sent = lax.optimization_barrier((panels[1], sent))
    second, sent = reduce_row(turned(second), right)
    green, sent = lax.optimization_barrier((green_one, sent))
    sums = [first, second]
    src = source(owners, green, rows, width)
    rate = jnp.stack(sums) + src
    return rate.transpose(2, 0, 1, 3).astype(jnp.bfloat16)


def solution(mesh):
    fine = Mesh(mesh.devices.reshape(tuple(SIZES.values())), tuple(SIZES))
    return jax.shard_map(
        shards,
        mesh=fine,
        in_specs=(P("row", None, COL), P(COL, None, None, None, "row"), P(), P()),
        out_specs=P("row", None, None, COL),
        check_vma=False,
    )
```

```python
import jax
import jax.numpy as jnp
from jax import lax
from jax.sharding import Mesh, PartitionSpec as P

SIZES = {"y": 2, "z": 8, "x": 4, "core": 2, "row": 4}
COL = ("y", "z", "x", "core")
SLICES = 2


def pick(array, index):
    return lax.dynamic_index_in_dim(array, index, 0, keepdims=False)


def swap(array):
    return lax.ppermute(array, "core", [(0, 1), (1, 0)])


def scatter(panels, owner):
    depth = panels.shape[-1]
    core, x = owner % SIZES["core"], (owner // SIZES["core"]) % SIZES["x"]
    line = owner // (SIZES["core"] * SIZES["x"])
    parts = lax.all_to_all(panels.reshape(SIZES["core"] * SIZES["x"], -1, depth), ("core", "x"), 0, 0, tiled=True)
    part = pick(parts, core * SIZES["x"] + x).reshape(SIZES["z"], -1, depth)
    pieces = lax.all_to_all(jnp.concatenate([part] * SIZES["y"]), ("y", "z"), 0, 0, tiled=True)
    return pick(pieces, line)


def gather(piece):
    count = SIZES["x"] * SIZES["z"]
    return lax.all_to_all(jnp.broadcast_to(piece[None], (count,) + piece.shape), ("x", "z"), 0, 0, tiled=True)


def slab_product(panel, right):
    re, im = panel.reshape(2, -1, panel.shape[-1])
    left = jnp.stack([jnp.concatenate([im, re], axis=1), jnp.concatenate([-re, im], axis=1)])
    left = left.reshape(2, SIZES["row"], -1, left.shape[-1]).transpose(1, 0, 2, 3)
    flat = left.reshape(-1, left.shape[-1])
    product = jnp.dot(flat, right, preferred_element_type=jnp.float32).astype(jnp.bfloat16)
    return product.reshape(SIZES["row"], -1, right.shape[-1])


def chosen(index, count):
    return (index[:, None] == jnp.arange(count, dtype=jnp.int32)[None, :]).astype(jnp.float32)


def source(first, columns, green):
    orbitals = green.shape[1]

    def take(row_index, col_index):
        half = jnp.einsum("qi,cik->cqk", chosen(row_index, orbitals), green, precision="highest")
        return jnp.einsum("cqk,nk->cqn", half, chosen(col_index, orbitals), precision="highest")

    a = take(first // orbitals, columns // orbitals)
    b = take(first % orbitals, columns % orbitals)
    return jnp.stack([a[0] * b[0] - a[1] * b[1], a[0] * b[1] + a[1] * b[0]])


def shards(g2_block, panel_slots, owners, green_one):
    width = g2_block.shape[2]
    panel_rows = panel_slots.shape[3]
    rows = panel_rows // SIZES["row"]
    core = lax.axis_index("core")
    owner = pick(owners, core)
    mine = g2_block.transpose(1, 0, 2).reshape(-1, width)
    right = lax.optimization_barrier(jnp.concatenate([mine, swap(mine)], axis=1))
    piece = scatter(panel_slots[0], owner)
    piece_rows = piece.shape[0]
    cut = piece_rows // SLICES
    panels = [gather(piece[index * cut:(index + 1) * cut]) for index in range(SLICES)]

    product = slab_product(panels[0], right)
    early = lax.psum_scatter(product, "row", scatter_dimension=0, tiled=True)
    panel, product = lax.optimization_barrier((panels[1], product))
    product = slab_product(panel, right)
    green, _ = lax.optimization_barrier((green_one, product))
    late = lax.all_to_all(product, "row", 0, 0, tiled=True)

    first = (2 * owner + core) * panel_rows + lax.axis_index("row") * rows + jnp.arange(rows, dtype=jnp.int32)
    own = lax.axis_index(COL) * width + jnp.arange(width, dtype=jnp.int32)
    other = (lax.axis_index(COL) + 1 - 2 * core) * width + jnp.arange(width, dtype=jnp.int32)
    src = source(first, jnp.concatenate([own, other]), green)
    src = src.reshape(2, -1, SLICES, cut, 2 * width).transpose(2, 0, 1, 3, 4).reshape(SLICES, -1, 2 * width)

    sums = [early[0].astype(jnp.float32), jnp.sum(late.astype(jnp.float32), axis=0)]
    planes = []
    for index in range(SLICES):
        rate = (sums[index] + src[index]).astype(jnp.bfloat16)
        here = rate[:, :width]
        got = swap(rate[:, width:])
        planes.append(jnp.stack([jnp.where(core == 0, here, got), jnp.where(core == 0, got, here)]))
    rate = jnp.stack(planes).reshape(SLICES, 2, 2, -1, cut, width)
    return rate.transpose(3, 0, 4, 1, 2, 5).reshape(rows, 2, 2, width)


def solution(mesh):
    fine = Mesh(mesh.devices.reshape(tuple(SIZES.values())), tuple(SIZES))
    return jax.shard_map(
        shards,
        mesh=fine,
        in_specs=(P("row", None, COL), P(COL, None, None, None, "row"), P(), P()),
        out_specs=P("row", None, None, COL),
        check_vma=False,
    )
```

```python
import jax
import jax.numpy as jnp
from jax import lax
from jax.sharding import Mesh, PartitionSpec as P

NPAN = 2
SIZES = {"y": 2, "z": 8, "x": 4, "core": 2, "row": 4}
COL = ("y", "z", "x", "core")


def pick(array, index):
    return lax.dynamic_index_in_dim(array, index, 0, keepdims=False)


def shift(array, step):
    size = SIZES["row"]
    return lax.ppermute(array, "row", [(index, (index + step) % size) for index in range(size)])


def spread_pieces(panel):
    half = panel.shape[-1] // 2
    pieces = panel.reshape(-1, 8, 2, half).transpose(0, 2, 1, 3).reshape(-1, 8, half)
    return lax.all_to_all(pieces, COL, 0, 0, tiled=True)


def gather(piece):
    count = 2 * SIZES["y"] * SIZES["z"] * SIZES["x"]
    got = lax.all_to_all(jnp.broadcast_to(piece[None], (count,) + piece.shape), COL, 0, 0, tiled=True)
    return got.reshape(count // 2, 2, *piece.shape).transpose(0, 2, 1, 3).reshape(count * 4, -1)


def turned(panel):
    re, im = panel.reshape(2, -1, panel.shape[-1])
    full = jnp.stack([jnp.concatenate([im, re], axis=1), jnp.concatenate([-re, im], axis=1)])
    return full.reshape(2, SIZES["row"], -1, full.shape[-1]).transpose(1, 0, 2, 3)


def reduce_at_once(left, right):
    parts, _, rows, depth = left.shape
    product = jnp.dot(left.reshape(-1, depth), right, preferred_element_type=jnp.float32).astype(jnp.bfloat16)
    got = lax.all_to_all(product.reshape(parts, 2 * rows, -1), "row", 0, 0, tiled=True)
    return jnp.sum(got.astype(jnp.float32), axis=0).reshape(2, rows, -1), product


def reduce_row(left, right):
    row = lax.axis_index("row")
    rows = left.shape[2]

    def term(step):
        part = pick(left, (row + step) % SIZES["row"]).reshape(2 * rows, -1)
        part = jnp.dot(part, right, preferred_element_type=jnp.float32)
        return part.astype(jnp.bfloat16).astype(jnp.float32).reshape(2, rows, -1)

    far = term(2).astype(jnp.bfloat16)
    from_left = shift(far[0], 1).astype(jnp.float32)
    from_right = shift(far[1], -1).astype(jnp.float32)
    up, down = term(1), term(3)
    up = jnp.stack([up[0] + from_left, up[1]]).astype(jnp.bfloat16)
    down = jnp.stack([down[0], down[1] + from_right]).astype(jnp.bfloat16)
    sent = (up, down)
    own = term(0)
    up = shift(up, 1).astype(jnp.float32)
    down = shift(down, -1).astype(jnp.float32)
    return own + up + down, sent


def chosen(index, count):
    return (index[:, None] == jnp.arange(count, dtype=jnp.int32)[None, :]).astype(jnp.float32)


def source(owners, green, rows, width):
    orbitals = green.shape[1]
    first = (2 * owners + jnp.arange(NPAN, dtype=jnp.int32)) * (rows * SIZES["row"])
    pairs = first[:, None] + lax.axis_index("row") * rows + jnp.arange(rows, dtype=jnp.int32)[None, :]
    pairs = pairs.reshape(-1)
    columns = lax.axis_index(COL) * width + jnp.arange(width, dtype=jnp.int32)

    def take(row_index, col_index):
        half = jnp.einsum("qi,cik->cqk", chosen(row_index, orbitals), green, precision="highest")
        return jnp.einsum("cqk,nk->cqn", half, chosen(col_index, orbitals), precision="highest")

    a = take(pairs // orbitals, columns // orbitals)
    b = take(pairs % orbitals, columns % orbitals)
    re = a[0] * b[0] - a[1] * b[1]
    im = a[0] * b[1] + a[1] * b[0]
    return jnp.stack([re, im]).reshape(2, NPAN, rows, width).transpose(1, 0, 2, 3)


def shards(g2_block, panel_slots, owners, green_one):
    width = g2_block.shape[2]
    rows = panel_slots.shape[3] // SIZES["row"]
    right = g2_block.transpose(1, 0, 2).reshape(-1, width)
    panels = panel_slots[0].reshape(NPAN, -1, panel_slots.shape[-1])
    owned = jnp.where(lax.axis_index(COL) == owners[0], panels[0], panels[1])
    got = spread_pieces(owned)
    panel = gather(pick(got, owners[0]))
    got, panel = lax.optimization_barrier((got, panel))
    piece = lax.cond(
        owners[0] == owners[1],
        lambda: lax.optimization_barrier(pick(spread_pieces(panels[1]), owners[1])),
        lambda: lax.optimization_barrier(pick(got, owners[1])),
    )
    piece, panel = lax.optimization_barrier((piece, panel))
    second = gather(piece)
    first, sent = reduce_row(turned(panel), right)
    second, sent = lax.optimization_barrier((second, sent))
    second, sent = reduce_at_once(turned(second), right)
    green, sent = lax.optimization_barrier((green_one, sent))
    sums = [first, second]
    src = source(owners, green, rows, width)
    rate = jnp.stack(sums) + src
    return rate.transpose(2, 0, 1, 3).astype(jnp.bfloat16)


def solution(mesh):
    fine = Mesh(mesh.devices.reshape(tuple(SIZES.values())), tuple(SIZES))
    return jax.shard_map(
        shards,
        mesh=fine,
        in_specs=(P("row", None, COL), P(COL, None, None, None, "row"), P(), P()),
        out_specs=P("row", None, None, COL),
        check_vma=False,
    )
```

```python
import jax
import jax.numpy as jnp
from jax import lax
from jax.sharding import Mesh, PartitionSpec as P

NPAN = 2
SIZES = {"y": 2, "z": 8, "x": 4, "core": 2, "row": 4}
COL = ("y", "z", "x", "core")


def pick(array, index):
    return lax.dynamic_index_in_dim(array, index, 0, keepdims=False)


def shift(array, step):
    size = SIZES["row"]
    return lax.ppermute(array, "row", [(index, (index + step) % size) for index in range(size)])


def spread_pieces(panel):
    half = panel.shape[-1] // 2
    pieces = panel.reshape(-1, 8, 2, half).transpose(0, 2, 1, 3).reshape(-1, 8, half)
    return lax.all_to_all(pieces, COL, 0, 0, tiled=True)


def gather(pieces):
    count = SIZES["y"] * SIZES["z"] * SIZES["x"]
    copies = jnp.broadcast_to(pieces[None], (count,) + pieces.shape)
    own = lax.all_to_all(copies, ("y", "z", "x"), 0, 0, tiled=True)
    other = lax.ppermute(own, "core", [(0, 1), (1, 0)])
    return [half.transpose(1, 0, 2, 3).reshape(NPAN, -1, half.shape[-1]) for half in (own, other)]


def turned(panel):
    re, im = panel.reshape(2, -1, panel.shape[-1])
    full = jnp.stack([jnp.concatenate([im, re], axis=1), jnp.concatenate([-re, im], axis=1)])
    full = full.reshape(2, SIZES["row"], -1, full.shape[-1]).transpose(1, 0, 2, 3)
    return full.reshape(SIZES["row"], -1, full.shape[-1])


def reduce_row(lefts, right):
    row = lax.axis_index("row")

    def term(index, step):
        left = pick(lefts[index], (row + step) % SIZES["row"])
        return jnp.dot(left, right, preferred_element_type=jnp.float32).astype(jnp.bfloat16)

    def with_term(array, index, step):
        return (array.astype(jnp.float32) + term(index, step).astype(jnp.float32)).astype(jnp.bfloat16)

    far = [shift(term(0, 2), 1), shift(term(1, 2), -1)]
    straight = [shift(term(0, 3), -1), shift(term(1, 1), 1)]
    joined = [shift(with_term(far[0], 0, 1), 1), shift(with_term(far[1], 1, 3), -1)]
    own = [term(index, 0) for index in range(NPAN)]
    return [
        own[index].astype(jnp.float32) + straight[index].astype(jnp.float32) + joined[index].astype(jnp.float32)
        for index in range(NPAN)
    ]


def chosen(index, count):
    return (index[:, None] == jnp.arange(count, dtype=jnp.int32)[None, :]).astype(jnp.float32)


def source(owners, green, rows, width):
    orbitals = green.shape[1]
    first = (2 * owners + jnp.arange(NPAN, dtype=jnp.int32)) * (rows * SIZES["row"])
    pairs = first[:, None] + lax.axis_index("row") * rows + jnp.arange(rows, dtype=jnp.int32)[None, :]
    pairs = pairs.reshape(-1)
    columns = lax.axis_index(COL) * width + jnp.arange(width, dtype=jnp.int32)

    def take(row_index, col_index):
        half = jnp.einsum("qi,cik->cqk", chosen(row_index, orbitals), green, precision="highest")
        return jnp.einsum("cqk,nk->cqn", half, chosen(col_index, orbitals), precision="highest")

    a = take(pairs // orbitals, columns // orbitals)
    b = take(pairs % orbitals, columns % orbitals)
    re = a[0] * b[0] - a[1] * b[1]
    im = a[0] * b[1] + a[1] * b[0]
    return jnp.stack([re, im]).reshape(2, NPAN, rows, width).transpose(1, 0, 2, 3)


def shards(g2_block, panel_slots, owners, green_one):
    depth, _, width = g2_block.shape
    rows = panel_slots.shape[3] // SIZES["row"]
    core = lax.axis_index("core")
    panels = panel_slots[0].reshape(NPAN, -1, depth)
    owned = jnp.where(lax.axis_index(COL) == owners[0], panels[0], panels[1])
    got = spread_pieces(owned)
    piece = lax.cond(
        owners[0] == owners[1],
        lambda: lax.optimization_barrier(pick(spread_pieces(panels[1]), owners[1])),
        lambda: lax.optimization_barrier(pick(got, owners[1])),
    )
    pieces = jnp.stack([pick(got, owners[0]), piece])
    halves = gather(pieces)
    lefts = [turned(jnp.concatenate([half[index] for half in halves], axis=1)) for index in range(NPAN)]
    green, g2_block, _ = lax.optimization_barrier((green_one, g2_block, pieces))
    src = source(owners, green, rows, width).reshape(NPAN, -1, width)
    split = g2_block.transpose(1, 0, 2).reshape(2, 2, -1, width)
    right = jnp.where(core == 0, split, split[:, ::-1]).reshape(-1, width)
    sums = reduce_row(lefts, right)
    rate = jnp.stack([(sums[index] + src[index]).astype(jnp.bfloat16) for index in range(NPAN)])
    return rate.reshape(NPAN, 2, rows, width).transpose(2, 0, 1, 3)


def solution(mesh):
    fine = Mesh(mesh.devices.reshape(tuple(SIZES.values())), tuple(SIZES))
    return jax.shard_map(
        shards,
        mesh=fine,
        in_specs=(P("row", None, COL), P(COL, None, None, None, "row"), P(), P()),
        out_specs=P("row", None, None, COL),
        check_vma=False,
    )
```

```python
import jax
import jax.numpy as jnp
from jax import lax
from jax.sharding import Mesh, PartitionSpec as P

NPAN = 2
SIZES = {"y": 2, "z": 8, "x": 4, "core": 2, "row": 4}
COL = ("y", "z", "x", "core")


def pick(array, index):
    return lax.dynamic_index_in_dim(array, index, 0, keepdims=False)


def shift(array, step):
    size = SIZES["row"]
    return lax.ppermute(array, "row", [(index, (index + step) % size) for index in range(size)])


def spread_pieces(panel):
    half = panel.shape[-1] // 2
    pieces = panel.reshape(-1, 8, 2, half).transpose(0, 2, 1, 3).reshape(-1, 8, half)
    return lax.all_to_all(pieces, COL, 0, 0, tiled=True)


def gather(pieces):
    count = SIZES["y"] * SIZES["z"] * SIZES["x"]
    copies = jnp.broadcast_to(pieces[None], (count,) + pieces.shape)
    own = lax.all_to_all(copies, ("y", "z", "x"), 0, 0, tiled=True)
    other = lax.ppermute(own, "core", [(0, 1), (1, 0)])
    return [half.transpose(1, 0, 2, 3).reshape(NPAN, -1, half.shape[-1]) for half in (own, other)]


def turned(panel):
    re, im = panel.reshape(2, -1, panel.shape[-1])
    full = jnp.stack([jnp.concatenate([im, re], axis=1), jnp.concatenate([-re, im], axis=1)])
    full = full.reshape(2, SIZES["row"], -1, full.shape[-1]).transpose(1, 0, 2, 3)
    return full.reshape(SIZES["row"], -1, full.shape[-1])


def reduce_row(lefts, right):
    row = lax.axis_index("row")

    def term(index, step):
        left = pick(lefts[index], (row + step) % SIZES["row"])
        return jnp.dot(left, right, preferred_element_type=jnp.float32).astype(jnp.bfloat16)

    def with_term(array, index, step):
        return (array.astype(jnp.float32) + term(index, step).astype(jnp.float32)).astype(jnp.bfloat16)

    far = lax.optimization_barrier([shift(term(0, 2), 1), shift(term(1, 2), -1)])
    straight = [shift(term(0, 3), -1), shift(term(1, 1), 1)]
    sent = [with_term(far[0], 0, 1), with_term(far[1], 1, 3)]
    joined = [shift(sent[0], 1), shift(sent[1], -1)]
    own = [term(index, 0) for index in range(NPAN)]
    sums = [
        own[index].astype(jnp.float32) + straight[index].astype(jnp.float32) + joined[index].astype(jnp.float32)
        for index in range(NPAN)
    ]
    return sums, sent


def chosen(index, count):
    return (index[:, None] == jnp.arange(count, dtype=jnp.int32)[None, :]).astype(jnp.float32)


def source(owners, green, rows, width):
    orbitals = green.shape[1]
    first = (2 * owners + jnp.arange(NPAN, dtype=jnp.int32)) * (rows * SIZES["row"])
    pairs = first[:, None] + lax.axis_index("row") * rows + jnp.arange(rows, dtype=jnp.int32)[None, :]
    pairs = pairs.reshape(-1)
    columns = lax.axis_index(COL) * width + jnp.arange(width, dtype=jnp.int32)

    def take(row_index, col_index):
        half = jnp.einsum("qi,cik->cqk", chosen(row_index, orbitals), green, precision="highest")
        return jnp.einsum("cqk,nk->cqn", half, chosen(col_index, orbitals), precision="highest")

    a = take(pairs // orbitals, columns // orbitals)
    b = take(pairs % orbitals, columns % orbitals)
    re = a[0] * b[0] - a[1] * b[1]
    im = a[0] * b[1] + a[1] * b[0]
    return jnp.stack([re, im]).reshape(2, NPAN, rows, width).transpose(1, 0, 2, 3)


def shards(g2_block, panel_slots, owners, green_one):
    depth, _, width = g2_block.shape
    rows = panel_slots.shape[3] // SIZES["row"]
    core = lax.axis_index("core")
    panels = panel_slots[0].reshape(NPAN, -1, depth)
    owner, owner_next = owners[0], owners[1]
    owned = jnp.where(lax.axis_index(COL) == owner, panels[0], panels[1])
    got = spread_pieces(owned)
    right = g2_block.transpose(1, 0, 2).reshape(-1, width)
    got, right = lax.optimization_barrier((got, right))
    both = owner == owner_next
    extra = lax.cond(
        both,
        lambda: lax.optimization_barrier(pick(spread_pieces(panels[1]), owner_next)),
        lambda: jnp.zeros(got.shape[1:], got.dtype),
    )
    halves = gather(jnp.stack([pick(got, owner), jnp.where(both, extra, pick(got, owner_next))]))
    lefts = []
    for index in range(NPAN):
        own, other = halves[0][index], halves[1][index]
        ordered = [jnp.where(core == 0, own, other), jnp.where(core == 0, other, own)]
        lefts.append(turned(jnp.concatenate(ordered, axis=1)))
    sums, sent = reduce_row(lefts, right)
    green, _ = lax.optimization_barrier((green_one, sent))
    src = source(owners, green, rows, width).reshape(NPAN, -1, width)
    rate = jnp.stack([(sums[index] + src[index]).astype(jnp.bfloat16) for index in range(NPAN)])
    return rate.reshape(NPAN, 2, rows, width).transpose(2, 0, 1, 3)


def solution(mesh):
    fine = Mesh(mesh.devices.reshape(tuple(SIZES.values())), tuple(SIZES))
    return jax.shard_map(
        shards,
        mesh=fine,
        in_specs=(P("row", None, COL), P(COL, None, None, None, "row"), P(), P()),
        out_specs=P("row", None, None, COL),
        check_vma=False,
    )
```

```python
import jax
import jax.numpy as jnp
from jax import lax
from jax.sharding import Mesh, PartitionSpec as P

NPAN = 2
SIZES = {"y": 2, "z": 8, "x": 4, "core": 2, "row": 4}
COL = ("y", "z", "x", "core")


def pick(array, index):
    return lax.dynamic_index_in_dim(array, index, 0, keepdims=False)


def shift(array, step):
    size = SIZES["row"]
    return lax.ppermute(array, "row", [(index, (index + step) % size) for index in range(size)])


def spread_pieces(panel):
    half = panel.shape[-1] // 2
    pieces = panel.reshape(-1, 8, 2, half).transpose(0, 2, 1, 3).reshape(-1, 8, half)
    return lax.all_to_all(pieces, COL, 0, 0, tiled=True)


def gather(pieces):
    count = SIZES["y"] * SIZES["z"] * SIZES["x"]
    copies = jnp.broadcast_to(pieces[None], (count,) + pieces.shape)
    own = lax.all_to_all(copies, ("y", "z", "x"), 0, 0, tiled=True)
    other = lax.ppermute(own, "core", [(0, 1), (1, 0)])
    return [half.transpose(1, 0, 2, 3).reshape(NPAN, -1, half.shape[-1]) for half in (own, other)]


def turned(panel):
    re, im = panel.reshape(2, -1, panel.shape[-1])
    full = jnp.stack([jnp.concatenate([im, re], axis=1), jnp.concatenate([-re, im], axis=1)])
    full = full.reshape(2, SIZES["row"], -1, full.shape[-1]).transpose(1, 0, 2, 3)
    return full.reshape(SIZES["row"], -1, full.shape[-1])


def reduce_row(lefts, right):
    row = lax.axis_index("row")

    def term(index, step):
        left = pick(lefts[index], (row + step) % SIZES["row"])
        return jnp.dot(left, right, preferred_element_type=jnp.float32).astype(jnp.bfloat16)

    def with_term(array, index, step):
        return (array.astype(jnp.float32) + term(index, step).astype(jnp.float32)).astype(jnp.bfloat16)

    far = [shift(term(0, 2), 1), shift(term(1, 2), -1)]
    far, sent = lax.optimization_barrier((far, [term(0, 3), term(1, 1)]))
    straight = [shift(sent[0], -1), shift(sent[1], 1)]
    sent = [with_term(far[0], 0, 1), with_term(far[1], 1, 3)]
    joined = [shift(sent[0], 1), shift(sent[1], -1)]
    own = [term(index, 0) for index in range(NPAN)]
    sums = [
        own[index].astype(jnp.float32) + straight[index].astype(jnp.float32) + joined[index].astype(jnp.float32)
        for index in range(NPAN)
    ]
    return sums, sent


def chosen(index, count):
    return (index[:, None] == jnp.arange(count, dtype=jnp.int32)[None, :]).astype(jnp.float32)


def source(owners, green, rows, width):
    orbitals = green.shape[1]
    first = (2 * owners + jnp.arange(NPAN, dtype=jnp.int32)) * (rows * SIZES["row"])
    pairs = first[:, None] + lax.axis_index("row") * rows + jnp.arange(rows, dtype=jnp.int32)[None, :]
    pairs = pairs.reshape(-1)
    columns = lax.axis_index(COL) * width + jnp.arange(width, dtype=jnp.int32)

    def take(row_index, col_index):
        half = jnp.einsum("qi,cik->cqk", chosen(row_index, orbitals), green, precision="highest")
        return jnp.einsum("cqk,nk->cqn", half, chosen(col_index, orbitals), precision="highest")

    a = take(pairs // orbitals, columns // orbitals)
    b = take(pairs % orbitals, columns % orbitals)
    re = a[0] * b[0] - a[1] * b[1]
    im = a[0] * b[1] + a[1] * b[0]
    return jnp.stack([re, im]).reshape(2, NPAN, rows, width).transpose(1, 0, 2, 3)


def shards(g2_block, panel_slots, owners, green_one):
    depth, _, width = g2_block.shape
    rows = panel_slots.shape[3] // SIZES["row"]
    core = lax.axis_index("core")
    panels = panel_slots[0].reshape(NPAN, -1, depth)
    owner, owner_next = owners[0], owners[1]
    owned = jnp.where(lax.axis_index(COL) == owner, panels[0], panels[1])
    got = spread_pieces(owned)
    right = g2_block.transpose(1, 0, 2).reshape(-1, width)
    got, right = lax.optimization_barrier((got, right))
    both = owner == owner_next
    extra = lax.cond(
        both,
        lambda: lax.optimization_barrier(pick(spread_pieces(panels[1]), owner_next)),
        lambda: jnp.zeros(got.shape[1:], got.dtype),
    )
    halves = gather(jnp.stack([pick(got, owner), jnp.where(both, extra, pick(got, owner_next))]))
    lefts = []
    for index in range(NPAN):
        own, other = halves[0][index], halves[1][index]
        ordered = [jnp.where(core == 0, own, other), jnp.where(core == 0, other, own)]
        lefts.append(turned(jnp.concatenate(ordered, axis=1)))
    sums, sent = reduce_row(lefts, right)
    green, _ = lax.optimization_barrier((green_one, sent))
    src = source(owners, green, rows, width).reshape(NPAN, -1, width)
    rate = jnp.stack([(sums[index] + src[index]).astype(jnp.bfloat16) for index in range(NPAN)])
    return rate.reshape(NPAN, 2, rows, width).transpose(2, 0, 1, 3)


def solution(mesh):
    fine = Mesh(mesh.devices.reshape(tuple(SIZES.values())), tuple(SIZES))
    return jax.shard_map(
        shards,
        mesh=fine,
        in_specs=(P("row", None, COL), P(COL, None, None, None, "row"), P(), P()),
        out_specs=P("row", None, None, COL),
        check_vma=False,
    )
```

```python
import jax
import jax.numpy as jnp
from jax import lax
from jax.sharding import Mesh, PartitionSpec as P

NPAN = 2
SIZES = {"y": 2, "z": 8, "x": 4, "core": 2, "row": 4}
COL = ("y", "z", "x", "core")


def pick(array, index):
    return lax.dynamic_index_in_dim(array, index, 0, keepdims=False)


def shift(array, step):
    size = SIZES["row"]
    return lax.ppermute(array, "row", [(index, (index + step) % size) for index in range(size)])


def spread_pieces(panel):
    half = panel.shape[-1] // 2
    pieces = panel.reshape(-1, 8, 2, half).transpose(0, 2, 1, 3).reshape(-1, 8, half)
    return lax.all_to_all(pieces, COL, 0, 0, tiled=True)


def gather(pieces):
    count = SIZES["y"] * SIZES["z"] * SIZES["x"]
    copies = jnp.broadcast_to(pieces[None], (count,) + pieces.shape)
    own = lax.all_to_all(copies, ("y", "z", "x"), 0, 0, tiled=True)
    other = lax.ppermute(own, "core", [(0, 1), (1, 0)])
    return [half.transpose(1, 0, 2, 3).reshape(NPAN, -1, half.shape[-1]) for half in (own, other)]


def turned(panel):
    re, im = panel.reshape(2, -1, panel.shape[-1])
    full = jnp.stack([jnp.concatenate([im, re], axis=1), jnp.concatenate([-re, im], axis=1)])
    full = full.reshape(2, SIZES["row"], -1, full.shape[-1]).transpose(1, 0, 2, 3)
    return full.reshape(SIZES["row"], -1, full.shape[-1])


def reduce_row(lefts, right):
    row = lax.axis_index("row")

    def term(index, step):
        left = pick(lefts[index], (row + step) % SIZES["row"])
        return jnp.dot(left, right, preferred_element_type=jnp.float32).astype(jnp.bfloat16)

    def with_term(array, index, step):
        return (array.astype(jnp.float32) + term(index, step).astype(jnp.float32)).astype(jnp.bfloat16)

    far = [shift(term(0, 2), 1), shift(term(1, 2), -1)]
    sent = [
        jnp.concatenate([with_term(far[0], 0, 1), term(1, 1)]),
        jnp.concatenate([term(0, 3), with_term(far[1], 1, 3)]),
    ]
    sent, lefts = lax.optimization_barrier((sent, lefts))
    from_left = shift(sent[0], 1).reshape(NPAN, -1, right.shape[1]).astype(jnp.float32)
    from_right = shift(sent[1], -1).reshape(NPAN, -1, right.shape[1]).astype(jnp.float32)
    sums = [term(index, 0).astype(jnp.float32) + from_left[index] + from_right[index] for index in range(NPAN)]
    return sums, sent


def chosen(index, count):
    return (index[:, None] == jnp.arange(count, dtype=jnp.int32)[None, :]).astype(jnp.float32)


def source(owners, green, rows, width):
    orbitals = green.shape[1]
    first = (2 * owners + jnp.arange(NPAN, dtype=jnp.int32)) * (rows * SIZES["row"])
    pairs = first[:, None] + lax.axis_index("row") * rows + jnp.arange(rows, dtype=jnp.int32)[None, :]
    pairs = pairs.reshape(-1)
    columns = lax.axis_index(COL) * width + jnp.arange(width, dtype=jnp.int32)

    def take(row_index, col_index):
        half = jnp.einsum("qi,cik->cqk", chosen(row_index, orbitals), green, precision="highest")
        return jnp.einsum("cqk,nk->cqn", half, chosen(col_index, orbitals), precision="highest")

    a = take(pairs // orbitals, columns // orbitals)
    b = take(pairs % orbitals, columns % orbitals)
    re = a[0] * b[0] - a[1] * b[1]
    im = a[0] * b[1] + a[1] * b[0]
    return jnp.stack([re, im]).reshape(2, NPAN, rows, width).transpose(1, 0, 2, 3)


def shards(g2_block, panel_slots, owners, green_one):
    depth, _, width = g2_block.shape
    rows = panel_slots.shape[3] // SIZES["row"]
    core = lax.axis_index("core")
    panels = panel_slots[0].reshape(NPAN, -1, depth)
    owner, owner_next = owners[0], owners[1]
    owned = jnp.where(lax.axis_index(COL) == owner, panels[0], panels[1])
    got = spread_pieces(owned)
    right = g2_block.transpose(1, 0, 2).reshape(-1, width)
    got, right = lax.optimization_barrier((got, right))
    both = owner == owner_next
    extra = lax.cond(
        both,
        lambda: lax.optimization_barrier(pick(spread_pieces(panels[1]), owner_next)),
        lambda: jnp.zeros(got.shape[1:], got.dtype),
    )
    halves = gather(jnp.stack([pick(got, owner), jnp.where(both, extra, pick(got, owner_next))]))
    lefts = []
    for index in range(NPAN):
        own, other = halves[0][index], halves[1][index]
        ordered = [jnp.where(core == 0, own, other), jnp.where(core == 0, other, own)]
        lefts.append(turned(jnp.concatenate(ordered, axis=1)))
    sums, sent = reduce_row(lefts, right)
    green, _ = lax.optimization_barrier((green_one, sent))
    src = source(owners, green, rows, width).reshape(NPAN, -1, width)
    rate = jnp.stack([(sums[index] + src[index]).astype(jnp.bfloat16) for index in range(NPAN)])
    return rate.reshape(NPAN, 2, rows, width).transpose(2, 0, 1, 3)


def solution(mesh):
    fine = Mesh(mesh.devices.reshape(tuple(SIZES.values())), tuple(SIZES))
    return jax.shard_map(
        shards,
        mesh=fine,
        in_specs=(P("row", None, COL), P(COL, None, None, None, "row"), P(), P()),
        out_specs=P("row", None, None, COL),
        check_vma=False,
    )
```

```python
import jax
import jax.numpy as jnp
from jax import lax
from jax.sharding import Mesh, PartitionSpec as P

NPAN = 2
SIZES = {"y": 2, "z": 8, "x": 4, "core": 2, "row": 4}
COL = ("y", "z", "x", "core")
CUTS = 2


def pick(array, index):
    return lax.dynamic_index_in_dim(array, index, 0, keepdims=False)


def shift(array, step):
    size = SIZES["row"]
    return lax.ppermute(array, "row", [(index, (index + step) % size) for index in range(size)])


def spread_pieces(panel):
    half = panel.shape[-1] // 2
    pieces = panel.reshape(-1, 8, 2, half).transpose(0, 2, 1, 3).reshape(-1, 8, half)
    return lax.all_to_all(pieces, COL, 0, 0, tiled=True)


def gather(pieces):
    count = SIZES["y"] * SIZES["z"] * SIZES["x"]
    copies = jnp.broadcast_to(pieces[None], (count,) + pieces.shape)
    own = lax.all_to_all(copies, ("y", "z", "x"), 0, 0, tiled=True)
    other = lax.ppermute(own, "core", [(0, 1), (1, 0)])
    return [half.transpose(1, 0, 2, 3).reshape(NPAN, -1, half.shape[-1]) for half in (own, other)]


def turned(panel):
    re, im = panel.reshape(2, -1, panel.shape[-1])
    full = jnp.stack([jnp.concatenate([im, re], axis=1), jnp.concatenate([-re, im], axis=1)])
    full = full.reshape(2, SIZES["row"], -1, full.shape[-1]).transpose(1, 0, 2, 3)
    return full.reshape(SIZES["row"], -1, full.shape[-1])


def reduce_row(lefts, right):
    row = lax.axis_index("row")

    def term(index, step):
        left = pick(lefts[index], (row + step) % SIZES["row"])
        return jnp.dot(left, right, preferred_element_type=jnp.float32).astype(jnp.bfloat16)

    def with_term(array, index, step):
        return (array.astype(jnp.float32) + term(index, step).astype(jnp.float32)).astype(jnp.bfloat16)

    far = [shift(term(0, 2), 1), shift(term(1, 2), -1)]
    sent = [
        jnp.concatenate([with_term(far[0], 0, 1), term(1, 1)]),
        jnp.concatenate([term(0, 3), with_term(far[1], 1, 3)]),
    ]
    sent, lefts = lax.optimization_barrier((sent, lefts))
    arrived = [shift(sent[0], 1), shift(sent[1], -1)]
    own = [term(index, 0) for index in range(NPAN)]
    return own, [array.reshape(NPAN, -1, right.shape[1]) for array in arrived], sent


def chosen(index, count):
    return (index[:, None] == jnp.arange(count, dtype=jnp.int32)[None, :]).astype(jnp.float32)


def source(owners, green, rows, width):
    orbitals = green.shape[1]
    first = (2 * owners + jnp.arange(NPAN, dtype=jnp.int32)) * (rows * SIZES["row"])
    pairs = first[:, None] + lax.axis_index("row") * rows + jnp.arange(rows, dtype=jnp.int32)[None, :]
    pairs = pairs.reshape(-1)
    columns = lax.axis_index(COL) * width + jnp.arange(width, dtype=jnp.int32)

    def take(row_index, col_index):
        half = jnp.einsum("qi,cik->cqk", chosen(row_index, orbitals), green, precision="highest")
        return jnp.einsum("cqk,nk->cqn", half, chosen(col_index, orbitals), precision="highest")

    a = take(pairs // orbitals, columns // orbitals)
    b = take(pairs % orbitals, columns % orbitals)
    re = a[0] * b[0] - a[1] * b[1]
    im = a[0] * b[1] + a[1] * b[0]
    return jnp.stack([re, im]).reshape(2, NPAN, rows, width).transpose(1, 0, 2, 3)


def shards(g2_block, panel_slots, owners, green_one):
    depth, _, width = g2_block.shape
    rows = panel_slots.shape[3] // SIZES["row"]
    core = lax.axis_index("core")
    panels = panel_slots[0].reshape(NPAN, -1, depth)
    owner, owner_next = owners[0], owners[1]
    owned = jnp.where(lax.axis_index(COL) == owner, panels[0], panels[1])
    got = spread_pieces(owned)
    right = g2_block.transpose(1, 0, 2).reshape(-1, width)
    got, right = lax.optimization_barrier((got, right))
    both = owner == owner_next
    extra = lax.cond(
        both,
        lambda: lax.optimization_barrier(pick(spread_pieces(panels[1]), owner_next)),
        lambda: jnp.zeros(got.shape[1:], got.dtype),
    )
    halves = gather(jnp.stack([pick(got, owner), jnp.where(both, extra, pick(got, owner_next))]))
    lefts = []
    for index in range(NPAN):
        own, other = halves[0][index], halves[1][index]
        ordered = [jnp.where(core == 0, own, other), jnp.where(core == 0, other, own)]
        lefts.append(turned(jnp.concatenate(ordered, axis=1)))
    parts = [reduce_row(lefts, side) for side in jnp.split(right, CUTS, axis=1)]
    green, _ = lax.optimization_barrier((green_one, [part[2] for part in parts]))
    src = source(owners, green, rows, width).reshape(NPAN, -1, width)
    base = [jnp.concatenate([part[0][index] for part in parts], axis=1) for index in range(NPAN)]
    base = lax.optimization_barrier([base[index].astype(jnp.float32) + src[index] for index in range(NPAN)])
    rates = []
    for index in range(NPAN):
        rate = base[index]
        for side in range(2):
            arrived = jnp.concatenate([part[1][side][index] for part in parts], axis=1)
            rate = rate + arrived.astype(jnp.float32)
        rates.append(rate.astype(jnp.bfloat16))
    return jnp.stack(rates).reshape(NPAN, 2, rows, width).transpose(2, 0, 1, 3)


def solution(mesh):
    fine = Mesh(mesh.devices.reshape(tuple(SIZES.values())), tuple(SIZES))
    return jax.shard_map(
        shards,
        mesh=fine,
        in_specs=(P("row", None, COL), P(COL, None, None, None, "row"), P(), P()),
        out_specs=P("row", None, None, COL),
        check_vma=False,
    )
```

```python
import jax
import jax.numpy as jnp
from jax import lax
from jax.sharding import Mesh, PartitionSpec as P

NPAN = 2
SIZES = {"y": 2, "z": 8, "x": 4, "core": 2, "row": 4}
COL = ("y", "z", "x", "core")
CUTS = 1


def pick(array, index):
    return lax.dynamic_index_in_dim(array, index, 0, keepdims=False)


def shift(array, step):
    size = SIZES["row"]
    return lax.ppermute(array, "row", [(index, (index + step) % size) for index in range(size)])


def spread_pieces(panel):
    half = panel.shape[-1] // 2
    pieces = panel.reshape(-1, 8, 2, half).transpose(0, 2, 1, 3).reshape(-1, 8, half)
    return lax.all_to_all(pieces, COL, 0, 0, tiled=True)


def gather(pieces):
    count = SIZES["y"] * SIZES["z"] * SIZES["x"]
    copies = jnp.broadcast_to(pieces[None], (count,) + pieces.shape)
    own = lax.all_to_all(copies, ("y", "z", "x"), 0, 0, tiled=True)
    other = lax.ppermute(own, "core", [(0, 1), (1, 0)])
    return [half.transpose(1, 0, 2, 3).reshape(NPAN, -1, half.shape[-1]) for half in (own, other)]


def turned(panel):
    re, im = panel.reshape(2, -1, panel.shape[-1])
    full = jnp.stack([jnp.concatenate([im, re], axis=1), jnp.concatenate([-re, im], axis=1)])
    full = full.reshape(2, SIZES["row"], -1, full.shape[-1]).transpose(1, 0, 2, 3)
    return full.reshape(SIZES["row"], -1, full.shape[-1])


def reduce_row(lefts, right):
    row = lax.axis_index("row")

    def term(index, step):
        left = pick(lefts[index], (row + step) % SIZES["row"])
        return jnp.dot(left, right, preferred_element_type=jnp.float32).astype(jnp.bfloat16)

    def with_term(array, index, step):
        return (array.astype(jnp.float32) + term(index, step).astype(jnp.float32)).astype(jnp.bfloat16)

    far = [shift(term(0, 2), 1), shift(term(1, 2), -1)]
    sent = [
        jnp.concatenate([with_term(far[0], 0, 1), term(1, 1)]),
        jnp.concatenate([term(0, 3), with_term(far[1], 1, 3)]),
    ]
    sent, lefts = lax.optimization_barrier((sent, lefts))
    arrived = [shift(sent[0], 1), shift(sent[1], -1)]
    own = [term(index, 0) for index in range(NPAN)]
    return own, [array.reshape(NPAN, -1, right.shape[1]) for array in arrived], sent


def chosen(index, count):
    return (index[:, None] == jnp.arange(count, dtype=jnp.int32)[None, :]).astype(jnp.float32)


def source(owners, green, rows, width):
    orbitals = green.shape[1]
    first = (2 * owners + jnp.arange(NPAN, dtype=jnp.int32)) * (rows * SIZES["row"])
    pairs = first[:, None] + lax.axis_index("row") * rows + jnp.arange(rows, dtype=jnp.int32)[None, :]
    pairs = pairs.reshape(-1)
    columns = lax.axis_index(COL) * width + jnp.arange(width, dtype=jnp.int32)

    def take(row_index, col_index):
        half = jnp.einsum("qi,cik->cqk", chosen(row_index, orbitals), green, precision="highest")
        return jnp.einsum("cqk,nk->cqn", half, chosen(col_index, orbitals), precision="highest")

    a = take(pairs // orbitals, columns // orbitals)
    b = take(pairs % orbitals, columns % orbitals)
    re = a[0] * b[0] - a[1] * b[1]
    im = a[0] * b[1] + a[1] * b[0]
    return jnp.stack([re, im]).reshape(2, NPAN, rows, width).transpose(1, 0, 2, 3)


def shards(g2_block, panel_slots, owners, green_one):
    depth, _, width = g2_block.shape
    rows = panel_slots.shape[3] // SIZES["row"]
    core = lax.axis_index("core")
    panels = panel_slots[0].reshape(NPAN, -1, depth)
    owner, owner_next = owners[0], owners[1]
    owned = jnp.where(lax.axis_index(COL) == owner, panels[0], panels[1])
    got = spread_pieces(owned)
    right = g2_block.transpose(1, 0, 2).reshape(-1, width)
    got, right = lax.optimization_barrier((got, right))
    both = owner == owner_next
    extra = lax.cond(
        both,
        lambda: lax.optimization_barrier(pick(spread_pieces(panels[1]), owner_next)),
        lambda: jnp.zeros(got.shape[1:], got.dtype),
    )
    halves = gather(jnp.stack([pick(got, owner), jnp.where(both, extra, pick(got, owner_next))]))
    lefts = []
    for index in range(NPAN):
        own, other = halves[0][index], halves[1][index]
        ordered = [jnp.where(core == 0, own, other), jnp.where(core == 0, other, own)]
        lefts.append(turned(jnp.concatenate(ordered, axis=1)))
    parts = [reduce_row(lefts, side) for side in jnp.split(right, CUTS, axis=1)]
    green, _ = lax.optimization_barrier((green_one, [part[2] for part in parts]))
    src = source(owners, green, rows, width).reshape(NPAN, -1, width)
    base = [jnp.concatenate([part[0][index] for part in parts], axis=1) for index in range(NPAN)]
    base = lax.optimization_barrier([base[index].astype(jnp.float32) + src[index] for index in range(NPAN)])
    rates = []
    for index in range(NPAN):
        rate = base[index]
        for side in range(2):
            arrived = jnp.concatenate([part[1][side][index] for part in parts], axis=1)
            rate = rate + arrived.astype(jnp.float32)
        rates.append(rate.astype(jnp.bfloat16))
    return jnp.stack(rates).reshape(NPAN, 2, rows, width).transpose(2, 0, 1, 3)


def solution(mesh):
    fine = Mesh(mesh.devices.reshape(tuple(SIZES.values())), tuple(SIZES))
    return jax.shard_map(
        shards,
        mesh=fine,
        in_specs=(P("row", None, COL), P(COL, None, None, None, "row"), P(), P()),
        out_specs=P("row", None, None, COL),
        check_vma=False,
    )
```

```python
import jax
import jax.numpy as jnp
from jax import lax
from jax.sharding import Mesh, PartitionSpec as P

NPAN = 2
SIZES = {"y": 2, "z": 8, "x": 4, "core": 2, "row": 4}
COL = ("y", "z", "x", "core")


def pick(array, index):
    return lax.dynamic_index_in_dim(array, index, 0, keepdims=False)


def shift(array, step):
    size = SIZES["row"]
    return lax.ppermute(array, "row", [(index, (index + step) % size) for index in range(size)])


def spread_pieces(panel):
    half = panel.shape[-1] // 2
    pieces = panel.reshape(-1, 8, 2, half).transpose(0, 2, 1, 3).reshape(-1, 8, half)
    return lax.all_to_all(pieces, COL, 0, 0, tiled=True)


def gather(pieces):
    count = SIZES["y"] * SIZES["z"] * SIZES["x"]
    copies = jnp.broadcast_to(pieces[None], (count,) + pieces.shape)
    own = lax.all_to_all(copies, ("y", "z", "x"), 0, 0, tiled=True)
    other = lax.ppermute(own, "core", [(0, 1), (1, 0)])
    return [half.transpose(1, 0, 2, 3).reshape(NPAN, -1, half.shape[-1]) for half in (own, other)]


def turned(panel):
    re, im = panel.reshape(2, -1, panel.shape[-1])
    full = jnp.stack([jnp.concatenate([im, re], axis=1), jnp.concatenate([-re, im], axis=1)])
    full = full.reshape(2, SIZES["row"], -1, full.shape[-1]).transpose(1, 0, 2, 3)
    return full.reshape(SIZES["row"], -1, full.shape[-1])


def reduce_row(lefts, right):
    row = lax.axis_index("row")

    def term(index, step):
        left = pick(lefts[index], (row + step) % SIZES["row"])
        return jnp.dot(left, right, preferred_element_type=jnp.float32).astype(jnp.bfloat16)

    def with_term(array, index, step):
        return (array.astype(jnp.float32) + term(index, step).astype(jnp.float32)).astype(jnp.bfloat16)

    far = [shift(term(0, 2), 1), shift(term(1, 2), -1)]
    sent = [
        jnp.concatenate([with_term(far[0], 0, 1), term(1, 1)]),
        jnp.concatenate([term(0, 3), with_term(far[1], 1, 3)]),
    ]
    sent, lefts = lax.optimization_barrier((sent, lefts))
    from_left = shift(sent[0], 1).reshape(NPAN, -1, right.shape[1]).astype(jnp.float32)
    from_right = shift(sent[1], -1).reshape(NPAN, -1, right.shape[1]).astype(jnp.float32)
    sums = [term(index, 0).astype(jnp.float32) + from_left[index] + from_right[index] for index in range(NPAN)]
    return sums, sent


def chosen(index, count):
    return (index[:, None] == jnp.arange(count, dtype=jnp.int32)[None, :]).astype(jnp.float32)


def source(owners, green, rows, width):
    orbitals = green.shape[1]
    first = (2 * owners + jnp.arange(NPAN, dtype=jnp.int32)) * (rows * SIZES["row"])
    pairs = first[:, None] + lax.axis_index("row") * rows + jnp.arange(rows, dtype=jnp.int32)[None, :]
    pairs = pairs.reshape(-1)
    columns = lax.axis_index(COL) * width + jnp.arange(width, dtype=jnp.int32)

    def take(row_index, col_index):
        half = jnp.einsum("qi,cik->cqk", chosen(row_index, orbitals), green, precision="highest")
        return jnp.einsum("cqk,nk->cqn", half, chosen(col_index, orbitals), precision="highest")

    a = take(pairs // orbitals, columns // orbitals)
    b = take(pairs % orbitals, columns % orbitals)
    re = a[0] * b[0] - a[1] * b[1]
    im = a[0] * b[1] + a[1] * b[0]
    return jnp.stack([re, im]).reshape(2, NPAN, rows, width).transpose(1, 0, 2, 3)


def shards(g2_block, panel_slots, owners, green_one):
    depth, _, width = g2_block.shape
    rows = panel_slots.shape[3] // SIZES["row"]
    core = lax.axis_index("core")
    panels = panel_slots[0].reshape(NPAN, -1, depth)
    owner, owner_next = owners[0], owners[1]
    owned = pick(panels, jnp.where(lax.axis_index(COL) == owner, 0, 1))
    got = spread_pieces(owned)
    right = g2_block.transpose(1, 0, 2).reshape(-1, width)
    got, right = lax.optimization_barrier((got, right))
    both = owner == owner_next
    extra = lax.cond(
        both,
        lambda: lax.optimization_barrier(pick(spread_pieces(panels[1]), owner_next)),
        lambda: jnp.zeros(got.shape[1:], got.dtype),
    )
    halves = gather(jnp.stack([pick(got, owner), jnp.where(both, extra, pick(got, owner_next))]))
    lefts = []
    for index in range(NPAN):
        own, other = halves[0][index], halves[1][index]
        ordered = [jnp.where(core == 0, own, other), jnp.where(core == 0, other, own)]
        lefts.append(turned(jnp.concatenate(ordered, axis=1)))
    sums, sent = reduce_row(lefts, right)
    green, _ = lax.optimization_barrier((green_one, sent))
    src = source(owners, green, rows, width).reshape(NPAN, -1, width)
    rate = jnp.stack([(sums[index] + src[index]).astype(jnp.bfloat16) for index in range(NPAN)])
    return rate.reshape(NPAN, 2, rows, width).transpose(2, 0, 1, 3)


def solution(mesh):
    fine = Mesh(mesh.devices.reshape(tuple(SIZES.values())), tuple(SIZES))
    return jax.shard_map(
        shards,
        mesh=fine,
        in_specs=(P("row", None, COL), P(COL, None, None, None, "row"), P(), P()),
        out_specs=P("row", None, None, COL),
        check_vma=False,
    )
```
